32 devices in a mesh: dp: 8 (over z, y), ctx: 4 (over x, core).
Axes of the slice: x: 2, y: 2, z: 4, core: 2. Of those that a mesh axis runs over, the one named last changes fastest.
Arguments:
- query_rows: bfloat16 [8192, 8192], P(('dp', 'ctx')), may hold values from -34 to 34
- key_rows: bfloat16 [8192, 1024], P(('dp', 'ctx')), may hold values from -10 to 10, as said below
- value_rows: bfloat16 [8192, 1024], P(('dp', 'ctx')), may hold values from -6 to 6
- grad_out: bfloat16 [8192, 8192], P(('dp', 'ctx')), may hold values from -6 to 6
- dest_rows: int32 [8192], P(('dp', 'ctx')), may hold values from 0 to 8191, as said below
- key_blocks: int32 [8, 8, 4], P('dp', 'ctx'), may hold values from 0 to 7, as said below
- key_count: int32 [8, 8], P('dp', 'ctx'), may hold values from 1 to 4, as said below
Outputs:
- attn_out: bfloat16 [8192, 8192], P(('dp', 'ctx'))
- grad_query: bfloat16 [8192, 8192], P(('dp', 'ctx'))
- grad_key: bfloat16 [8192, 1024], P(('dp', 'ctx'))
- grad_value: bfloat16 [8192, 1024], P(('dp', 'ctx'))
The draws below stay inside these ranges and needn't reach their ends.
Inputs may be any that keep to these rules, and one draw needn't show every extreme that they name: `dest_rows`: A permutation of the learner rows; the 256 engine rows of each device hold exactly 8 rows for each device's 256 learner rows. `key_blocks`: each packed sequence is a run of token trees: a prompt of one or two blocks followed by two to four responses of one or two blocks each, the last tree possibly cut; the first tree has a prompt of two blocks and a first response of two blocks. For query block b the used entries, in increasing order, are the prompt blocks of b's tree and the blocks of b's own branch up to b itself; unused entries equal b. `key_count`: each packed sequence has a block that attends to 4 blocks. `key_rows`: keys of all heads.
All inputs are finite; a program needn't handle non-finite values.
Results may differ from the reference program's by a relative error of at most 0.02.
Values may be sent and summed in bfloat16 or wider, within the bound.
A program may use at most 192 MiB of HBM per device.

```python
import jax
import jax.numpy as jnp
from jax import lax

QH = 64
KVH = 8
HD = 128
BLK = 128
KL = 4
TOK_DEV = 256
SEQ = 1024
NB = 8
TOKENS = 8192
CAP = 8
N_DP = 8
N_CTX = 4


def draw_query_rows(key, part):
    noise_part = jnp.clip(jax.random.normal(jax.random.fold_in(key, 1), (TOKENS, QH * HD), jnp.float32), -4.0, 4.0)
    values_out = noise_part
    return values_out.astype(jnp.bfloat16)


def draw_key_rows(key, part):
    noise_part = jnp.clip(jax.random.normal(jax.random.fold_in(key, 4), (TOKENS, KVH * HD), jnp.float32), -4.0, 4.0)
    values_out = noise_part
    return values_out.astype(jnp.bfloat16)


def draw_dest_rows(key, part):
    devices_all = N_DP * N_CTX
    learner_perm = jax.vmap(lambda sub_key: jax.random.permutation(sub_key, TOK_DEV))(jax.random.split(jax.random.fold_in(key, 21), devices_all)).astype(jnp.int32)
    by_sender = learner_perm.reshape(devices_all, devices_all, CAP)
    offsets = (jnp.arange(devices_all, dtype=jnp.int32) * TOK_DEV)[:, None, None]
    by_sender = jnp.transpose(by_sender + offsets, (1, 0, 2)).reshape(devices_all, TOK_DEV)
    sender_perm = jax.vmap(lambda sub_key: jax.random.permutation(sub_key, TOK_DEV))(jax.random.split(jax.random.fold_in(key, 22), devices_all)).astype(jnp.int32)
    rows_index = jnp.arange(devices_all, dtype=jnp.int32)[:, None]
    placed = jnp.zeros((devices_all, TOK_DEV), jnp.int32).at[rows_index, sender_perm].set(by_sender)
    return placed.reshape(TOKENS)


def tree_one(sub_key):
    coins = jax.random.randint(sub_key, (NB, 3), 0, 6).astype(jnp.int32)
    slot_range = jnp.arange(KL, dtype=jnp.int32)

    def advance(carry, inputs):
        prompt_first, prompt_last, resp_first, left_over, kind_now, resp_left = carry
        block_index, coin_row = inputs
        prompt_len = jnp.where(block_index == 0, 2, 1 + coin_row[0] % 2)
        resp_draw = 1 + coin_row[1] % 2
        tree_width = 2 + coin_row[2] % 3
        is_new = left_over == 0
        after_prompt = is_new & (kind_now == 0)
        next_resp = is_new & (kind_now == 1) & (resp_left > 0)
        new_prompt = is_new & (kind_now == 1) & (resp_left == 0)
        resp_len = jnp.where((prompt_first == 0) & after_prompt, 2, resp_draw)
        prompt_first = jnp.where(new_prompt, block_index, prompt_first)
        prompt_last = jnp.where(after_prompt, block_index - 1, prompt_last)
        resp_first = jnp.where(after_prompt | next_resp, block_index, resp_first)
        kind_next = jnp.where(new_prompt, 0, jnp.where(is_new, 1, kind_now))
        left_next = jnp.where(new_prompt, prompt_len - 1, jnp.where(is_new, resp_len - 1, left_over - 1))
        resp_next = jnp.where(new_prompt, tree_width, jnp.where(after_prompt | next_resp, resp_left - 1, resp_left))
        prompt_count = jnp.where(kind_next == 0, 0, prompt_last - prompt_first + 1)
        branch_first = jnp.where(kind_next == 0, prompt_first, resp_first)
        list_count = prompt_count + block_index - branch_first + 1
        entries = jnp.where(slot_range < prompt_count, prompt_first + slot_range, branch_first + slot_range - prompt_count)
        entries = jnp.where(slot_range < list_count, entries, block_index)
        carry_next = (prompt_first, prompt_last, resp_first, left_next, kind_next, resp_next)
        return (carry_next, (entries.astype(jnp.int32), list_count.astype(jnp.int32)))
    start = (jnp.int32(0), jnp.int32(0), jnp.int32(0), jnp.int32(0), jnp.int32(1), jnp.int32(0))
    ignored, outputs = lax.scan(advance, start, (jnp.arange(NB, dtype=jnp.int32), coins))
    return outputs


def tree_lists(key):
    return jax.vmap(tree_one)(jax.random.split(jax.random.fold_in(key, 11), N_DP))


def draw_key_blocks(key, part):
    return tree_lists(key)[0]


def draw_key_count(key, part):
    return tree_lists(key)[1]


def block_levels(stream_key, extent, cuts, least, high):
    loudness, own = 1.0, jax.random.fold_in(stream_key, 6)
    for position, shards_of in cuts:
        steps = jnp.exp(jax.random.uniform(jax.random.fold_in(own, position), (shards_of,), jnp.float32, least / len(cuts), high / len(cuts)))
        loudness = loudness * jnp.repeat(steps, extent[position] // shards_of).reshape([-1 if axis == position else 1 for axis in range(len(extent))])
    return loudness


def noise(key, extent, deviation, limit, cuts=(), held_as=jnp.bfloat16):
    gain = block_levels(key, extent, cuts, -0.22, 0.18) if cuts else 1.0
    values = jax.random.normal(key, extent, jnp.float32) * deviation * gain
    return jnp.minimum(jnp.maximum(values, -limit), limit).astype(held_as)


def setup_inputs(seed: int = 0) -> dict:
    streams_of = jax.random.split(jax.random.key(seed), 8)
    query_rows = draw_query_rows(jax.random.fold_in(streams_of[7], 71), 0)
    key_rows = draw_key_rows(jax.random.fold_in(streams_of[7], 71), 0)
    value_rows = noise(streams_of[2], (TOKENS, KVH * HD), 1.0, 6.0, ((0, 32),))
    grad_out = noise(streams_of[3], (TOKENS, QH * HD), 1.0, 6.0, ((0, 32),))
    dest_rows = draw_dest_rows(jax.random.fold_in(streams_of[7], 71), 0)
    key_blocks = draw_key_blocks(jax.random.fold_in(streams_of[7], 71), 0)
    key_count = draw_key_count(jax.random.fold_in(streams_of[7], 71), 0)
    return dict(query_rows=query_rows, key_rows=key_rows, value_rows=value_rows, grad_out=grad_out, dest_rows=dest_rows, key_blocks=key_blocks, key_count=key_count)


def attend(query_block, grad_block, key_all, value_all, block_list, list_count, block_index):
    span = KL * BLK
    groups = QH // KVH
    scaling = 1.0 / (HD ** 0.5)
    key_sel = key_all[block_list].reshape(span, KVH, HD).astype(jnp.float32)
    value_sel = value_all[block_list].reshape(span, KVH, HD).astype(jnp.float32)
    query_heads = query_block.reshape(BLK, KVH, groups, HD).astype(jnp.float32)
    grad_heads = grad_block.reshape(BLK, KVH, groups, HD).astype(jnp.float32)
    slot_index = jnp.arange(span, dtype=jnp.int32) // BLK
    is_valid = slot_index < list_count
    is_own = block_list[slot_index] == block_index
    query_pos = jnp.arange(BLK, dtype=jnp.int32)[:, None]
    key_pos = (jnp.arange(span, dtype=jnp.int32) % BLK)[None, :]
    allowed = is_valid[None, :] & (jnp.logical_not(is_own)[None, :] | (query_pos >= key_pos))
    scores = jnp.einsum("qhgd,khd->hgqk", query_heads, key_sel) * scaling
    scores = jnp.where(allowed, scores, -jnp.inf)
    row_max = jnp.max(scores, axis=-1, keepdims=True)
    weights = jnp.exp(scores - row_max)
    probability = weights / jnp.sum(weights, axis=-1, keepdims=True)
    prob_low = probability.astype(jnp.bfloat16).astype(jnp.float32)
    output = jnp.einsum("hgqk,khd->qhgd", prob_low, value_sel).astype(jnp.bfloat16)
    row_delta = jnp.sum(grad_heads * output.astype(jnp.float32), axis=-1)
    row_delta = jnp.transpose(row_delta, (1, 2, 0))[..., None]
    grad_probs = jnp.einsum("qhgd,khd->hgqk", grad_heads, value_sel)
    grad_scores = (probability * (grad_probs - row_delta)).astype(jnp.bfloat16).astype(jnp.float32)
    grad_query = (jnp.einsum("hgqk,khd->qhgd", grad_scores, key_sel) * scaling).astype(jnp.bfloat16)
    grad_key = jnp.einsum("hgqk,qhgd->khd", grad_scores, query_heads) * scaling
    grad_value = jnp.einsum("hgqk,qhgd->khd", prob_low, grad_heads)
    return (output.reshape(BLK, QH * HD), grad_query.reshape(BLK, QH * HD),
            grad_key.reshape(KL, BLK, KVH * HD), grad_value.reshape(KL, BLK, KVH * HD))


def group_pass(inputs):
    query_seq, key_seq, value_seq, grad_seq, block_lists, list_counts = inputs
    key_all = key_seq.reshape(NB, BLK, KVH * HD)
    value_all = value_seq.reshape(NB, BLK, KVH * HD)

    def one_block(block_inputs):
        query_block, grad_block, block_list, list_count, block_index = block_inputs
        return attend(query_block, grad_block, key_all, value_all, block_list, list_count, block_index)

    output, grad_query, key_parts, value_parts = lax.map(one_block, (
        query_seq.reshape(NB, BLK, QH * HD), grad_seq.reshape(NB, BLK, QH * HD),
        block_lists, list_counts, jnp.arange(NB, dtype=jnp.int32)))
    grad_key = jnp.zeros((NB, BLK, KVH * HD), jnp.float32).at[block_lists].add(key_parts)
    grad_value = jnp.zeros((NB, BLK, KVH * HD), jnp.float32).at[block_lists].add(value_parts)
    return (output.reshape(SEQ, QH * HD), grad_query.reshape(SEQ, QH * HD),
            grad_key.reshape(SEQ, KVH * HD).astype(jnp.bfloat16),
            grad_value.reshape(SEQ, KVH * HD).astype(jnp.bfloat16))


def reference(query_rows, key_rows, value_rows, grad_out, dest_rows, key_blocks, key_count):
    query_learn = jnp.zeros_like(query_rows).at[dest_rows].set(query_rows)
    key_learn = jnp.zeros_like(key_rows).at[dest_rows].set(key_rows)
    value_learn = jnp.zeros_like(value_rows).at[dest_rows].set(value_rows)
    grad_learn = jnp.zeros_like(grad_out).at[dest_rows].set(grad_out)
    groups_count = TOKENS // SEQ
    output, grad_query, grad_key, grad_value = lax.map(group_pass, (
        query_learn.reshape(groups_count, SEQ, QH * HD),
        key_learn.reshape(groups_count, SEQ, KVH * HD),
        value_learn.reshape(groups_count, SEQ, KVH * HD),
        grad_learn.reshape(groups_count, SEQ, QH * HD),
        key_blocks, key_count))
    return (output.reshape(TOKENS, QH * HD), grad_query.reshape(TOKENS, QH * HD),
            grad_key.reshape(TOKENS, KVH * HD), grad_value.reshape(TOKENS, KVH * HD))
```

```python
import functools
import math

import jax
import jax.numpy as jnp
from jax import lax
from jax.experimental import pallas as pl
from jax.experimental.pallas import tpu as pltpu
from jax.sharding import PartitionSpec as P

HD = 128
BLK = 128
F32 = jnp.float32
BF16 = jnp.bfloat16
VMEM_LIMIT = 48 * 1024 * 1024


def chunk_sizes(heads):
    sizes, left = [], heads
    while left:
        sizes.append(2 if left > 2 else 1)
        left -= sizes[-1]
    return sizes


def dot(a, b, ca, cb):
    return lax.dot_general(a, b, (((ca,), (cb,)), ((), ())), preferred_element_type=F32)


def send_order(dest_col, dest_row):
    rows = dest_col.shape[0]
    rank = jnp.sum((dest_col < dest_row).astype(jnp.int32), axis=0, keepdims=True)
    place = lax.broadcasted_iota(jnp.int32, (rows, rows), 0)
    return (place == rank).astype(F32).astype(BF16)


def prep_kv_kernel(col_ref, row_ref, key_ref, value_ref, out_ref):
    rows, width = key_ref.shape
    dest = col_ref[...]
    perm = send_order(dest, row_ref[...])
    out_ref[:, 0:width] = dot(perm, key_ref[...], 1, 0).astype(BF16)
    out_ref[:, width : 2 * width] = dot(perm, value_ref[...], 1, 0).astype(BF16)
    slot = jnp.broadcast_to(lax.rem(dest, rows), (rows, HD))
    lane = lax.broadcasted_iota(jnp.int32, (rows, HD), 1)
    digits = jnp.where(lane == 0, slot & 127, slot >> 7).astype(F32).astype(BF16)
    out_ref[:, 2 * width :] = dot(perm, digits, 1, 0).astype(BF16)


def prep_qg_kernel(col_ref, row_ref, query_ref, grad_ref, out_ref):
    width = query_ref.shape[1]
    perm = send_order(col_ref[...], row_ref[...])
    out_ref[:, 0:width] = dot(perm, query_ref[...], 1, 0).astype(BF16)
    out_ref[:, width:] = dot(perm, grad_ref[...], 1, 0).astype(BF16)


def place_kernel(recv_ref, out_ref, perm_ref):
    rows, width = out_ref.shape
    slot = recv_ref[:, width : width + 1].astype(F32) + 128.0 * recv_ref[
        :, width + 1 : width + 2
    ].astype(F32)
    target = lax.broadcasted_iota(jnp.int32, (rows, rows), 1).astype(F32)
    perm = jnp.transpose((target == slot).astype(F32)).astype(BF16)
    perm_ref[...] = perm
    out_ref[...] = dot(perm, recv_ref[:, 0:width], 1, 0).astype(BF16)


def attend_kernel(
    groups, slots, blocks_ref, count_ref, base_ref, perm_ref, qg_ref, key_ref, value_ref, *rest
):
    out_ref, dq_ref, dkv_ref, q_scr, g_scr, dk_scr, dv_scr = rest[-7:]
    rows = perm_ref.shape[0]
    width = groups * HD
    span = slots * BLK
    perm = perm_ref[...]
    q_scr[...] = dot(perm, qg_ref[:, 0:width], 1, 0).astype(BF16)
    g_scr[...] = dot(perm, qg_ref[:, width:], 1, 0).astype(BF16)
    dk_scr[...] = jnp.zeros_like(dk_scr)
    dv_scr[...] = jnp.zeros_like(dv_scr)
    scaling = 1.0 / math.sqrt(HD)
    scale2 = scaling * math.log2(math.e)
    pair = 2
    diff = lax.broadcasted_iota(jnp.int32, (BLK, BLK), 1) - lax.broadcasted_iota(
        jnp.int32, (BLK, BLK), 0
    )
    for b in range(rows // BLK):
        own = base_ref[0] + b
        count = count_ref[b]
        bias, starts = [], []
        for s in range(slots):
            blk = blocks_ref[b * slots + s]
            level = jnp.where(s < count, jnp.where(blk == own, 0, -BLK), BLK)
            bias.append(jnp.where(diff >= level, 0.0, -jnp.inf).astype(F32))
            starts.append(pl.multiple_of(blk * BLK, BLK))
        bias = jnp.concatenate(bias, axis=0)
        bias = jnp.concatenate([bias] * pair, axis=1)
        key_sel = jnp.concatenate([key_ref[pl.ds(at, BLK), :] for at in starts], axis=0)
        value_sel = jnp.concatenate([value_ref[pl.ds(at, BLK), :] for at in starts], axis=0)
        key_t = jnp.transpose(key_sel.astype(F32)).astype(BF16)
        value_t = jnp.transpose(value_sel.astype(F32)).astype(BF16)
        r0 = b * BLK
        dk = jnp.zeros((span, HD), F32)
        dv = jnp.zeros((span, HD), F32)
        for h in range(0, groups, pair):
            cols = [slice((h + i) * HD, (h + i + 1) * HD) for i in range(pair)]
            q2 = jnp.concatenate([q_scr[r0 : r0 + BLK, c] for c in cols], axis=0)
            g2 = jnp.concatenate([g_scr[r0 : r0 + BLK, c] for c in cols], axis=0)
            s_t = dot(key_sel, q2, 1, 1) * scale2 + bias
            dp_t = dot(value_sel, g2, 1, 1)
            e_t = jnp.exp2(s_t - jnp.max(s_t, axis=0, keepdims=True))
            p_t = e_t * (1.0 / jnp.sum(e_t, axis=0, keepdims=True))
            pb_t = p_t.astype(BF16)
            o_t = dot(value_t, pb_t, 1, 0)
            o_low = o_t.astype(BF16).astype(F32)
            delta = jnp.sum(jnp.transpose(g2.astype(F32)) * o_low, axis=0, keepdims=True)
            ds_t = (p_t * (dp_t - delta)).astype(BF16)
            dq_t = dot(key_t, ds_t, 1, 0) * scaling
            o_n = jnp.transpose(o_low).astype(BF16)
            dq_n = jnp.transpose(dq_t).astype(BF16)
            for i, c in enumerate(cols):
                out_ref[r0 : r0 + BLK, c] = o_n[i * BLK : (i + 1) * BLK]
                dq_ref[r0 : r0 + BLK, c] = dq_n[i * BLK : (i + 1) * BLK]
            dk = dk + dot(ds_t, q2, 1, 0)
            dv = dv + dot(pb_t, g2, 1, 0)
        for s, at in enumerate(starts):
            dk_scr[pl.ds(at, BLK), :] += dk[s * BLK : (s + 1) * BLK]
            dv_scr[pl.ds(at, BLK), :] += dv[s * BLK : (s + 1) * BLK]
    dkv_ref[:, 0:HD] = (dk_scr[...] * scaling).astype(BF16)
    dkv_ref[:, HD:] = dv_scr[...].astype(BF16)


def body(query_rows, key_rows, value_rows, grad_out, dest_rows, key_blocks, key_count):
    peers = lax.axis_size("dp") * lax.axis_size("ctx")
    rows, q_width = query_rows.shape
    kv_width = key_rows.shape[1]
    kv_heads = kv_width // HD
    groups = q_width // kv_width
    head_width = groups * HD
    local_blocks, slots = key_blocks.shape[1:]
    seq = rows * lax.axis_size("ctx")
    dest_col = dest_rows.reshape(rows, 1)
    dest_row = dest_rows.reshape(1, rows)
    params = pltpu.CompilerParams(vmem_limit_bytes=VMEM_LIMIT)

    def exchange(x):
        y = lax.all_to_all(
            x.reshape(peers, rows // peers, x.shape[1]),
            ("dp", "ctx"),
            split_axis=0,
            concat_axis=0,
            tiled=True,
        )
        return y.reshape(rows, x.shape[1])

    sent_kv = pl.pallas_call(
        prep_kv_kernel,
        out_shape=jax.ShapeDtypeStruct((rows, 2 * kv_width + HD), BF16),
        compiler_params=params,
        name="prep_kv",
    )(dest_col, dest_row, key_rows, value_rows)
    recv_kv = exchange(sent_kv)

    sizes = chunk_sizes(kv_heads)
    received = []
    first = 0
    for size in sizes:
        sent = pl.pallas_call(
            prep_qg_kernel,
            grid=(size,),
            in_specs=[
                pl.BlockSpec((rows, 1), lambda j: (0, 0)),
                pl.BlockSpec((1, rows), lambda j: (0, 0)),
                pl.BlockSpec((rows, head_width), lambda j, f=first: (0, f + j)),
                pl.BlockSpec((rows, head_width), lambda j, f=first: (0, f + j)),
            ],
            out_specs=pl.BlockSpec((rows, 2 * head_width), lambda j: (0, j)),
            out_shape=jax.ShapeDtypeStruct((rows, size * 2 * head_width), BF16),
            compiler_params=params,
            cost_estimate=pl.CostEstimate(
                flops=4 * rows * rows * size * head_width,
                bytes_accessed=8 * rows * size * head_width,
                transcendentals=0,
            ),
            name="prep_qg",
        )(dest_col, dest_row, query_rows, grad_out)
        received.append(exchange(sent))
        first += size

    placed, perm = pl.pallas_call(
        place_kernel,
        out_shape=(
            jax.ShapeDtypeStruct((rows, 2 * kv_width), BF16),
            jax.ShapeDtypeStruct((rows, rows), BF16),
        ),
        compiler_params=params,
        name="place_kv",
    )(recv_kv)
    kv_all = lax.all_gather(placed, "ctx", axis=0, tiled=True)

    block_list = key_blocks.reshape(local_blocks * slots)
    counts = key_count.reshape(local_blocks)
    base = (lax.axis_index("ctx") * local_blocks).astype(jnp.int32).reshape(1)
    out = dq = None
    sums = []
    first = 0
    for size, recv in zip(sizes, received):
        operands = [perm, recv, kv_all, kv_all]
        in_specs = [
            pl.BlockSpec((rows, rows), lambda j, *_: (0, 0)),
            pl.BlockSpec((rows, 2 * head_width), lambda j, *_: (0, j)),
            pl.BlockSpec((seq, HD), lambda j, *_, f=first: (0, f + j)),
            pl.BlockSpec((seq, HD), lambda j, *_, f=first: (0, kv_heads + f + j)),
        ]
        aliases = {}
        if out is not None:
            aliases = {7: 0, 8: 1}
            operands += [out, dq]
            in_specs += [pl.BlockSpec(memory_space=pl.ANY)] * 2
        out, dq, dkv = pl.pallas_call(
            functools.partial(attend_kernel, groups, slots),
            grid_spec=pltpu.PrefetchScalarGridSpec(
                num_scalar_prefetch=3,
                grid=(size,),
                in_specs=in_specs,
                out_specs=[
                    pl.BlockSpec((rows, head_width), lambda j, *_, f=first: (0, f + j)),
                    pl.BlockSpec((rows, head_width), lambda j, *_, f=first: (0, f + j)),
                    pl.BlockSpec((seq, 2 * HD), lambda j, *_: (0, j)),
                ],
                scratch_shapes=[
                    pltpu.VMEM((rows, head_width), BF16),
                    pltpu.VMEM((rows, head_width), BF16),
                    pltpu.VMEM((seq, HD), F32),
                    pltpu.VMEM((seq, HD), F32),
                ],
            ),
            out_shape=(
                jax.ShapeDtypeStruct((rows, q_width), BF16),
                jax.ShapeDtypeStruct((rows, q_width), BF16),
                jax.ShapeDtypeStruct((seq, size * 2 * HD), BF16),
            ),
            input_output_aliases=aliases,
            compiler_params=params,
            cost_estimate=pl.CostEstimate(
                flops=20 * rows * slots * BLK * size * head_width,
                bytes_accessed=8 * rows * size * head_width + 8 * seq * size * HD,
                transcendentals=rows * slots * BLK * size * groups,
            ),
            name="attend",
        )(block_list, counts, base, *operands)
        sums.append(lax.psum_scatter(dkv, "ctx", scatter_dimension=0, tiled=True))
        first += size

    total = jnp.concatenate(sums, axis=1).reshape(rows, kv_heads, 2, HD)
    return (
        out,
        dq,
        total[:, :, 0].reshape(rows, kv_width),
        total[:, :, 1].reshape(rows, kv_width),
    )


def solution(mesh):
    split = P(("dp", "ctx"), None)
    return jax.shard_map(
        body,
        mesh=mesh,
        in_specs=(
            split,
            split,
            split,
            split,
            P(("dp", "ctx")),
            P("dp", "ctx", None),
            P("dp", "ctx"),
        ),
        out_specs=(split, split, split, split),
        check_vma=False,
    )
```

```python
import functools
import math

import jax
import jax.numpy as jnp
from jax import lax
from jax.experimental import pallas as pl
from jax.experimental.pallas import tpu as pltpu
from jax.sharding import PartitionSpec as P

HD = 128
BLK = 128
F32 = jnp.float32
BF16 = jnp.bfloat16
VMEM_LIMIT = 60 * 1024 * 1024


def chunk_sizes(heads):
    sizes, left = [], heads
    while left:
        sizes.append(min(len(sizes) + 1, left))
        left -= sizes[-1]
    return sizes[::-1]


def dot(a, b, ca, cb):
    return lax.dot_general(a, b, (((ca,), (cb,)), ((), ())), preferred_element_type=F32)


def send_order(dest_col, dest_row):
    rows = dest_col.shape[0]
    rank = jnp.sum((dest_col < dest_row).astype(jnp.int32), axis=0, keepdims=True)
    place = lax.broadcasted_iota(jnp.int32, (rows, rows), 0)
    return (place == rank).astype(F32).astype(BF16)


def prep_first_kernel(size, col_ref, row_ref, query_ref, grad_ref, key_ref, value_ref, out_ref):
    rows, width = key_ref.shape
    head_width = query_ref.shape[1] // size
    dest = col_ref[...]
    perm = send_order(dest, row_ref[...])

    def put(at, values):
        out_ref[:, at : at + values.shape[1]] = dot(perm, values, 1, 0).astype(BF16)
        return at + values.shape[1]

    at = 0
    for j in range(size):
        at = put(at, query_ref[:, j * head_width : (j + 1) * head_width])
        at = put(at, grad_ref[:, j * head_width : (j + 1) * head_width])
    at = put(at, key_ref[...])
    at = put(at, value_ref[...])
    slot = jnp.broadcast_to(lax.rem(dest, rows), (rows, HD))
    lane = lax.broadcasted_iota(jnp.int32, (rows, HD), 1)
    put(at, jnp.where(lane == 0, slot & 127, slot >> 7).astype(F32).astype(BF16))


def prep_qg_kernel(col_ref, row_ref, query_ref, grad_ref, out_ref):
    width = query_ref.shape[1]
    perm = send_order(col_ref[...], row_ref[...])
    out_ref[:, 0:width] = dot(perm, query_ref[...], 1, 0).astype(BF16)
    out_ref[:, width:] = dot(perm, grad_ref[...], 1, 0).astype(BF16)


def place_kernel(recv_ref, out_ref, perm_ref):
    rows, width = out_ref.shape
    end = recv_ref.shape[1] - HD
    slot = recv_ref[:, end : end + 1].astype(F32) + 128.0 * recv_ref[
        :, end + 1 : end + 2
    ].astype(F32)
    target = lax.broadcasted_iota(jnp.int32, (rows, rows), 1).astype(F32)
    perm = jnp.transpose((target == slot).astype(F32)).astype(BF16)
    perm_ref[...] = perm
    out_ref[...] = dot(perm, recv_ref[:, end - width : end], 1, 0).astype(BF16)


def finish_kernel(sizes, *refs):
    dk_ref, dv_ref = refs[-2:]
    rows = dk_ref.shape[0]
    head = 0
    for size, ref in zip(sizes, refs):
        total = ref[0:rows, :].astype(F32)
        for part in range(1, ref.shape[0] // rows):
            total = total + ref[part * rows : (part + 1) * rows, :].astype(F32)
        total = total.astype(BF16)
        for j in range(size):
            cols = slice(head * HD, (head + 1) * HD)
            dk_ref[:, cols] = total[:, 2 * j * HD : (2 * j + 1) * HD]
            dv_ref[:, cols] = total[:, (2 * j + 1) * HD : (2 * j + 2) * HD]
            head += 1


def attend_kernel(
    groups, slots, blocks_ref, count_ref, base_ref, perm_ref, qg_ref, key_ref, value_ref, *rest
):
    out_ref, dq_ref, dkv_ref, q_scr, g_scr, dk_scr, dv_scr = rest[-7:]
    rows = perm_ref.shape[0]
    width = groups * HD
    span = slots * BLK
    perm = perm_ref[...]
    q_scr[...] = dot(perm, qg_ref[:, 0:width], 1, 0).astype(BF16)
    g_scr[...] = dot(perm, qg_ref[:, width:], 1, 0).astype(BF16)
    dk_scr[...] = jnp.zeros_like(dk_scr)
    dv_scr[...] = jnp.zeros_like(dv_scr)
    scaling = 1.0 / math.sqrt(HD)
    scale2 = scaling * math.log2(math.e)
    pair = 2
    diff = lax.broadcasted_iota(jnp.int32, (BLK, BLK), 1) - lax.broadcasted_iota(
        jnp.int32, (BLK, BLK), 0
    )
    for b in range(rows // BLK):
        own = base_ref[0] + b
        count = count_ref[b]
        bias, starts = [], []
        for s in range(slots):
            blk = blocks_ref[b * slots + s]
            level = jnp.where(s < count, jnp.where(blk == own, 0, -BLK), BLK)
            bias.append(jnp.where(diff >= level, 0.0, -jnp.inf).astype(F32))
            starts.append(pl.multiple_of(blk * BLK, BLK))
        bias = jnp.concatenate(bias, axis=0)
        bias = jnp.concatenate([bias] * pair, axis=1)
        key_sel = jnp.concatenate([key_ref[pl.ds(at, BLK), :] for at in starts], axis=0)
        value_sel = jnp.concatenate([value_ref[pl.ds(at, BLK), :] for at in starts], axis=0)
        key_t = jnp.transpose(key_sel.astype(F32)).astype(BF16)
        value_t = jnp.transpose(value_sel.astype(F32)).astype(BF16)
        r0 = b * BLK
        dk = jnp.zeros((span, HD), F32)
        dv = jnp.zeros((span, HD), F32)
        for h in range(0, groups, pair):
            cols = [slice((h + i) * HD, (h + i + 1) * HD) for i in range(pair)]
            q2 = jnp.concatenate([q_scr[r0 : r0 + BLK, c] for c in cols], axis=0)
            g2 = jnp.concatenate([g_scr[r0 : r0 + BLK, c] for c in cols], axis=0)
            s_t = dot(key_sel, q2, 1, 1) * scale2 + bias
            dp_t = dot(value_sel, g2, 1, 1)
            e_t = jnp.exp2(s_t - jnp.max(s_t, axis=0, keepdims=True))
            p_t = e_t * (1.0 / jnp.sum(e_t, axis=0, keepdims=True))
            pb_t = p_t.astype(BF16)
            o_t = dot(value_t, pb_t, 1, 0)
            o_low = o_t.astype(BF16).astype(F32)
            delta = jnp.sum(jnp.transpose(g2.astype(F32)) * o_low, axis=0, keepdims=True)
            ds_t = (p_t * (dp_t - delta)).astype(BF16)
            dq_t = dot(key_t, ds_t, 1, 0) * scaling
            o_n = jnp.transpose(o_low).astype(BF16)
            dq_n = jnp.transpose(dq_t).astype(BF16)
            for i, c in enumerate(cols):
                out_ref[r0 : r0 + BLK, c] = o_n[i * BLK : (i + 1) * BLK]
                dq_ref[r0 : r0 + BLK, c] = dq_n[i * BLK : (i + 1) * BLK]
            dk = dk + dot(ds_t, q2, 1, 0)
            dv = dv + dot(pb_t, g2, 1, 0)
        for s, at in enumerate(starts):
            dk_scr[pl.ds(at, BLK), :] += dk[s * BLK : (s + 1) * BLK]
            dv_scr[pl.ds(at, BLK), :] += dv[s * BLK : (s + 1) * BLK]
    dkv_ref[:, 0:HD] = (dk_scr[...] * scaling).astype(BF16)
    dkv_ref[:, HD:] = dv_scr[...].astype(BF16)


def body(query_rows, key_rows, value_rows, grad_out, dest_rows, key_blocks, key_count):
    peers = lax.axis_size("dp") * lax.axis_size("ctx")
    rows, q_width = query_rows.shape
    kv_width = key_rows.shape[1]
    kv_heads = kv_width // HD
    groups = q_width // kv_width
    head_width = groups * HD
    local_blocks, slots = key_blocks.shape[1:]
    seq = rows * lax.axis_size("ctx")
    dest_col = dest_rows.reshape(rows, 1)
    dest_row = dest_rows.reshape(1, rows)
    params = pltpu.CompilerParams(vmem_limit_bytes=VMEM_LIMIT)

    def exchange(x):
        y = lax.all_to_all(
            x.reshape(peers, rows // peers, x.shape[1]),
            ("dp", "ctx"),
            split_axis=0,
            concat_axis=0,
            tiled=True,
        )
        return y.reshape(rows, x.shape[1])

    sizes = chunk_sizes(kv_heads)
    head_cols = sizes[0] * head_width
    sent = pl.pallas_call(
        functools.partial(prep_first_kernel, sizes[0]),
        grid=(1,),
        in_specs=[
            pl.BlockSpec((rows, 1), lambda j: (0, 0)),
            pl.BlockSpec((1, rows), lambda j: (0, 0)),
            pl.BlockSpec((rows, head_cols), lambda j: (0, 0)),
            pl.BlockSpec((rows, head_cols), lambda j: (0, 0)),
            pl.BlockSpec((rows, kv_width), lambda j: (0, 0)),
            pl.BlockSpec((rows, kv_width), lambda j: (0, 0)),
        ],
        out_specs=pl.BlockSpec((rows, 2 * head_cols + 2 * kv_width + HD), lambda j: (0, 0)),
        out_shape=jax.ShapeDtypeStruct((rows, 2 * head_cols + 2 * kv_width + HD), BF16),
        compiler_params=params,
        name="prep_first",
    )(dest_col, dest_row, query_rows, grad_out, key_rows, value_rows)
    received = [exchange(sent)]
    first = sizes[0]
    for size in sizes[1:]:
        sent = pl.pallas_call(
            prep_qg_kernel,
            grid=(size,),
            in_specs=[
                pl.BlockSpec((rows, 1), lambda j: (0, 0)),
                pl.BlockSpec((1, rows), lambda j: (0, 0)),
                pl.BlockSpec((rows, head_width), lambda j, f=first: (0, f + j)),
                pl.BlockSpec((rows, head_width), lambda j, f=first: (0, f + j)),
            ],
            out_specs=pl.BlockSpec((rows, 2 * head_width), lambda j: (0, j)),
            out_shape=jax.ShapeDtypeStruct((rows, size * 2 * head_width), BF16),
            compiler_params=params,
            cost_estimate=pl.CostEstimate(
                flops=4 * rows * rows * size * head_width,
                bytes_accessed=8 * rows * size * head_width,
                transcendentals=0,
            ),
            name="prep_qg",
        )(dest_col, dest_row, query_rows, grad_out)
        received.append(exchange(sent))
        first += size

    placed, perm = pl.pallas_call(
        place_kernel,
        out_shape=(
            jax.ShapeDtypeStruct((rows, 2 * kv_width), BF16),
            jax.ShapeDtypeStruct((rows, rows), BF16),
        ),
        compiler_params=params,
        name="place_kv",
    )(received[0])
    kv_all = lax.all_gather(placed, "ctx", axis=0, tiled=True)

    block_list = key_blocks.reshape(local_blocks * slots)
    counts = key_count.reshape(local_blocks)
    base = (lax.axis_index("ctx") * local_blocks).astype(jnp.int32).reshape(1)
    out = dq = None
    sums = []
    first = 0
    for size, recv in zip(sizes, received):
        operands = [perm, recv, kv_all, kv_all]
        in_specs = [
            pl.BlockSpec((rows, rows), lambda j, *_: (0, 0)),
            pl.BlockSpec((rows, 2 * head_width), lambda j, *_: (0, j)),
            pl.BlockSpec((seq, HD), lambda j, *_, f=first: (0, f + j)),
            pl.BlockSpec((seq, HD), lambda j, *_, f=first: (0, kv_heads + f + j)),
        ]
        aliases = {}
        if out is not None:
            aliases = {7: 0, 8: 1}
            operands += [out, dq]
            in_specs += [pl.BlockSpec(memory_space=pl.ANY)] * 2
        out, dq, dkv = pl.pallas_call(
            functools.partial(attend_kernel, groups, slots),
            grid_spec=pltpu.PrefetchScalarGridSpec(
                num_scalar_prefetch=3,
                grid=(size,),
                in_specs=in_specs,
                out_specs=[
                    pl.BlockSpec((rows, head_width), lambda j, *_, f=first: (0, f + j)),
                    pl.BlockSpec((rows, head_width), lambda j, *_, f=first: (0, f + j)),
                    pl.BlockSpec((seq, 2 * HD), lambda j, *_: (0, j)),
                ],
                scratch_shapes=[
                    pltpu.VMEM((rows, head_width), BF16),
                    pltpu.VMEM((rows, head_width), BF16),
                    pltpu.VMEM((seq, HD), F32),
                    pltpu.VMEM((seq, HD), F32),
                ],
            ),
            out_shape=(
                jax.ShapeDtypeStruct((rows, q_width), BF16),
                jax.ShapeDtypeStruct((rows, q_width), BF16),
                jax.ShapeDtypeStruct((seq, size * 2 * HD), BF16),
            ),
            input_output_aliases=aliases,
            compiler_params=params,
            cost_estimate=pl.CostEstimate(
                flops=20 * rows * slots * BLK * size * head_width,
                bytes_accessed=8 * rows * size * head_width + 8 * seq * size * HD,
                transcendentals=rows * slots * BLK * size * groups,
            ),
            name="attend",
        )(block_list, counts, base, *operands)
        if first + size < kv_heads:
            sums.append(lax.psum_scatter(dkv, "ctx", scatter_dimension=0, tiled=True))
        else:
            sums.append(lax.all_to_all(dkv, "ctx", split_axis=0, concat_axis=0, tiled=True))
        first += size

    dk, dv = pl.pallas_call(
        functools.partial(finish_kernel, sizes),
        out_shape=(jax.ShapeDtypeStruct((rows, kv_width), BF16),) * 2,
        compiler_params=params,
        name="finish",
    )(*sums)
    return out, dq, dk, dv


def solution(mesh):
    split = P(("dp", "ctx"), None)
    return jax.shard_map(
        body,
        mesh=mesh,
        in_specs=(
            split,
            split,
            split,
            split,
            P(("dp", "ctx")),
            P("dp", "ctx", None),
            P("dp", "ctx"),
        ),
        out_specs=(split, split, split, split),
        check_vma=False,
    )
```

```python
import functools
import math

import jax
import jax.numpy as jnp
from jax import lax
from jax.experimental import pallas as pl
from jax.experimental.pallas import tpu as pltpu
from jax.sharding import PartitionSpec as P

HD = 128
BLK = 128
F32 = jnp.float32
BF16 = jnp.bfloat16
VMEM_LIMIT = 60 * 1024 * 1024


TAIL = 2


def chunk_sizes(heads):
    if heads < 4:
        return [1] * heads
    return [heads // 4, heads - heads // 4 - TAIL, 1, 1]


def dot(a, b, ca, cb):
    return lax.dot_general(a, b, (((ca,), (cb,)), ((), ())), preferred_element_type=F32)


def send_order(dest_col, dest_row):
    rows = dest_col.shape[0]
    rank = jnp.sum((dest_col < dest_row).astype(jnp.int32), axis=0, keepdims=True)
    place = lax.broadcasted_iota(jnp.int32, (rows, rows), 0)
    return (place == rank).astype(F32).astype(BF16)


def prep_first_kernel(size, col_ref, row_ref, query_ref, grad_ref, key_ref, value_ref, out_ref):
    rows, width = key_ref.shape
    head_width = query_ref.shape[1] // size
    dest = col_ref[...]
    perm = send_order(dest, row_ref[...])

    def put(at, values):
        out_ref[:, at : at + values.shape[1]] = dot(perm, values, 1, 0).astype(BF16)
        return at + values.shape[1]

    at = 0
    for j in range(size):
        at = put(at, query_ref[:, j * head_width : (j + 1) * head_width])
        at = put(at, grad_ref[:, j * head_width : (j + 1) * head_width])
    at = put(at, key_ref[...])
    at = put(at, value_ref[...])
    slot = jnp.broadcast_to(lax.rem(dest, rows), (rows, HD))
    lane = lax.broadcasted_iota(jnp.int32, (rows, HD), 1)
    put(at, jnp.where(lane == 0, slot & 127, slot >> 7).astype(F32).astype(BF16))


def prep_qg_kernel(col_ref, row_ref, query_ref, grad_ref, out_ref):
    width = query_ref.shape[1]
    perm = send_order(col_ref[...], row_ref[...])
    out_ref[:, 0:width] = dot(perm, query_ref[...], 1, 0).astype(BF16)
    out_ref[:, width:] = dot(perm, grad_ref[...], 1, 0).astype(BF16)


def place_kernel(recv_ref, out_ref, perm_ref):
    rows, width = out_ref.shape
    end = recv_ref.shape[1] - HD
    slot = recv_ref[:, end : end + 1].astype(F32) + 128.0 * recv_ref[
        :, end + 1 : end + 2
    ].astype(F32)
    target = lax.broadcasted_iota(jnp.int32, (rows, rows), 1).astype(F32)
    perm = jnp.transpose((target == slot).astype(F32)).astype(BF16)
    perm_ref[...] = perm
    out_ref[...] = dot(perm, recv_ref[:, end - width : end], 1, 0).astype(BF16)


def finish_kernel(sizes, *refs):
    dk_ref, dv_ref = refs[-2:]
    rows = dk_ref.shape[0]
    head = 0
    for size, ref in zip(sizes, refs):
        total = ref[0:rows, :].astype(F32)
        for part in range(1, ref.shape[0] // rows):
            total = total + ref[part * rows : (part + 1) * rows, :].astype(F32)
        total = total.astype(BF16)
        for j in range(size):
            cols = slice(head * HD, (head + 1) * HD)
            dk_ref[:, cols] = total[:, 2 * j * HD : (2 * j + 1) * HD]
            dv_ref[:, cols] = total[:, (2 * j + 1) * HD : (2 * j + 2) * HD]
            head += 1


def attend_kernel(
    groups, slots, blocks_ref, count_ref, base_ref, perm_ref, qg_ref, key_ref, value_ref, *rest
):
    out_ref, dq_ref, dkv_ref, q_scr, g_scr, dk_scr, dv_scr = rest[-7:]
    rows = perm_ref.shape[0]
    width = groups * HD
    span = slots * BLK
    perm = perm_ref[...]
    q_scr[...] = dot(perm, qg_ref[:, 0:width], 1, 0).astype(BF16)
    g_scr[...] = dot(perm, qg_ref[:, width:], 1, 0).astype(BF16)
    dk_scr[...] = jnp.zeros_like(dk_scr)
    dv_scr[...] = jnp.zeros_like(dv_scr)
    scaling = 1.0 / math.sqrt(HD)
    scale2 = scaling * math.log2(math.e)
    pair = 2
    diff = lax.broadcasted_iota(jnp.int32, (BLK, BLK), 1) - lax.broadcasted_iota(
        jnp.int32, (BLK, BLK), 0
    )
    for b in range(rows // BLK):
        own = base_ref[0] + b
        count = count_ref[b]
        bias, starts = [], []
        for s in range(slots):
            blk = blocks_ref[b * slots + s]
            level = jnp.where(s < count, jnp.where(blk == own, 0, -BLK), BLK)
            bias.append(jnp.where(diff >= level, 0.0, -jnp.inf).astype(F32))
            starts.append(pl.multiple_of(blk * BLK, BLK))
        bias = jnp.concatenate(bias, axis=0)
        bias = jnp.concatenate([bias] * pair, axis=1)
        key_sel = jnp.concatenate([key_ref[pl.ds(at, BLK), :] for at in starts], axis=0)
        value_sel = jnp.concatenate([value_ref[pl.ds(at, BLK), :] for at in starts], axis=0)
        key_t = jnp.transpose(key_sel.astype(F32)).astype(BF16)
        value_t = jnp.transpose(value_sel.astype(F32)).astype(BF16)
        r0 = b * BLK
        dk = jnp.zeros((span, HD), F32)
        dv = jnp.zeros((span, HD), F32)
        for h in range(0, groups, pair):
            cols = [slice((h + i) * HD, (h + i + 1) * HD) for i in range(pair)]
            q2 = jnp.concatenate([q_scr[r0 : r0 + BLK, c] for c in cols], axis=0)
            g2 = jnp.concatenate([g_scr[r0 : r0 + BLK, c] for c in cols], axis=0)
            s_t = dot(key_sel, q2, 1, 1) * scale2 + bias
            dp_t = dot(value_sel, g2, 1, 1)
            e_t = jnp.exp2(s_t - jnp.max(s_t, axis=0, keepdims=True))
            p_t = e_t * (1.0 / jnp.sum(e_t, axis=0, keepdims=True))
            pb_t = p_t.astype(BF16)
            o_t = dot(value_t, pb_t, 1, 0)
            o_low = o_t.astype(BF16).astype(F32)
            delta = jnp.sum(jnp.transpose(g2.astype(F32)) * o_low, axis=0, keepdims=True)
            ds_t = (p_t * (dp_t - delta)).astype(BF16)
            dq_t = dot(key_t, ds_t, 1, 0) * scaling
            o_n = jnp.transpose(o_low).astype(BF16)
            dq_n = jnp.transpose(dq_t).astype(BF16)
            for i, c in enumerate(cols):
                out_ref[r0 : r0 + BLK, c] = o_n[i * BLK : (i + 1) * BLK]
                dq_ref[r0 : r0 + BLK, c] = dq_n[i * BLK : (i + 1) * BLK]
            dk = dk + dot(ds_t, q2, 1, 0)
            dv = dv + dot(pb_t, g2, 1, 0)
        for s, at in enumerate(starts):
            dk_scr[pl.ds(at, BLK), :] += dk[s * BLK : (s + 1) * BLK]
            dv_scr[pl.ds(at, BLK), :] += dv[s * BLK : (s + 1) * BLK]
    dkv_ref[:, 0:HD] = (dk_scr[...] * scaling).astype(BF16)
    dkv_ref[:, HD:] = dv_scr[...].astype(BF16)


def body(query_rows, key_rows, value_rows, grad_out, dest_rows, key_blocks, key_count):
    peers = lax.axis_size("dp") * lax.axis_size("ctx")
    rows, q_width = query_rows.shape
    kv_width = key_rows.shape[1]
    kv_heads = kv_width // HD
    groups = q_width // kv_width
    head_width = groups * HD
    local_blocks, slots = key_blocks.shape[1:]
    seq = rows * lax.axis_size("ctx")
    dest_col = dest_rows.reshape(rows, 1)
    dest_row = dest_rows.reshape(1, rows)
    params = pltpu.CompilerParams(vmem_limit_bytes=VMEM_LIMIT)

    def exchange(x):
        y = lax.all_to_all(
            x.reshape(peers, rows // peers, x.shape[1]),
            ("dp", "ctx"),
            split_axis=0,
            concat_axis=0,
            tiled=True,
        )
        return y.reshape(rows, x.shape[1])

    sizes = chunk_sizes(kv_heads)
    head_cols = sizes[0] * head_width
    sent = pl.pallas_call(
        functools.partial(prep_first_kernel, sizes[0]),
        grid=(1,),
        in_specs=[
            pl.BlockSpec((rows, 1), lambda j: (0, 0)),
            pl.BlockSpec((1, rows), lambda j: (0, 0)),
            pl.BlockSpec((rows, head_cols), lambda j: (0, 0)),
            pl.BlockSpec((rows, head_cols), lambda j: (0, 0)),
            pl.BlockSpec((rows, kv_width), lambda j: (0, 0)),
            pl.BlockSpec((rows, kv_width), lambda j: (0, 0)),
        ],
        out_specs=pl.BlockSpec((rows, 2 * head_cols + 2 * kv_width + HD), lambda j: (0, 0)),
        out_shape=jax.ShapeDtypeStruct((rows, 2 * head_cols + 2 * kv_width + HD), BF16),
        compiler_params=params,
        name="prep_first",
    )(dest_col, dest_row, query_rows, grad_out, key_rows, value_rows)
    received = [exchange(sent)]
    placed, perm = pl.pallas_call(
        place_kernel,
        out_shape=(
            jax.ShapeDtypeStruct((rows, 2 * kv_width), BF16),
            jax.ShapeDtypeStruct((rows, rows), BF16),
        ),
        compiler_params=params,
        name="place_kv",
    )(received[0])
    kv_all = lax.all_gather(placed, "ctx", axis=0, tiled=True)

    def send(c):
        first, size = sum(sizes[:c]), sizes[c]
        return pl.pallas_call(
            prep_qg_kernel,
            grid=(size,),
            in_specs=[
                pl.BlockSpec((rows, 1), lambda j: (0, 0)),
                pl.BlockSpec((1, rows), lambda j: (0, 0)),
                pl.BlockSpec((rows, head_width), lambda j: (0, first + j)),
                pl.BlockSpec((rows, head_width), lambda j: (0, first + j)),
            ],
            out_specs=pl.BlockSpec((rows, 2 * head_width), lambda j: (0, j)),
            out_shape=jax.ShapeDtypeStruct((rows, size * 2 * head_width), BF16),
            compiler_params=params,
            cost_estimate=pl.CostEstimate(
                flops=4 * rows * rows * size * head_width,
                bytes_accessed=8 * rows * size * head_width,
                transcendentals=0,
            ),
            name="prep_qg",
        )(dest_col, dest_row, query_rows, grad_out)

    block_list = key_blocks.reshape(local_blocks * slots)
    counts = key_count.reshape(local_blocks)
    base = (lax.axis_index("ctx") * local_blocks).astype(jnp.int32).reshape(1)

    def attend(c, recv, out, dq, dkv, dkv_heads, dkv_first):
        first, size = sum(sizes[:c]), sizes[c]
        operands = [perm, recv, kv_all, kv_all]
        in_specs = [
            pl.BlockSpec((rows, rows), lambda j, *_: (0, 0)),
            pl.BlockSpec((rows, 2 * head_width), lambda j, *_: (0, j)),
            pl.BlockSpec((seq, HD), lambda j, *_: (0, first + j)),
            pl.BlockSpec((seq, HD), lambda j, *_: (0, kv_heads + first + j)),
        ]
        aliases = {}
        for place, array in enumerate((out, dq, dkv)):
            if array is not None:
                aliases[3 + len(operands)] = place
                operands.append(array)
                in_specs.append(pl.BlockSpec(memory_space=pl.ANY))
        return pl.pallas_call(
            functools.partial(attend_kernel, groups, slots),
            grid_spec=pltpu.PrefetchScalarGridSpec(
                num_scalar_prefetch=3,
                grid=(size,),
                in_specs=in_specs,
                out_specs=[
                    pl.BlockSpec((rows, head_width), lambda j, *_: (0, first + j)),
                    pl.BlockSpec((rows, head_width), lambda j, *_: (0, first + j)),
                    pl.BlockSpec((seq, 2 * HD), lambda j, *_: (0, dkv_first + j)),
                ],
                scratch_shapes=[
                    pltpu.VMEM((rows, head_width), BF16),
                    pltpu.VMEM((rows, head_width), BF16),
                    pltpu.VMEM((seq, HD), F32),
                    pltpu.VMEM((seq, HD), F32),
                ],
            ),
            out_shape=(
                jax.ShapeDtypeStruct((rows, q_width), BF16),
                jax.ShapeDtypeStruct((rows, q_width), BF16),
                jax.ShapeDtypeStruct((seq, dkv_heads * 2 * HD), BF16),
            ),
            input_output_aliases=aliases,
            compiler_params=params,
            cost_estimate=pl.CostEstimate(
                flops=20 * rows * slots * BLK * size * head_width,
                bytes_accessed=8 * rows * size * head_width + 8 * seq * size * HD,
                transcendentals=rows * slots * BLK * size * groups,
            ),
            name="attend",
        )(block_list, counts, base, *operands)

    chunks = len(sizes)
    tail_from = max(chunks - TAIL, 0)
    tail_sizes = sizes[tail_from:]
    sums = [None] * tail_from
    out = dq = tail = None
    for c in range(chunks):
        if c + 1 < chunks:
            sent = send(c + 1)
            if c >= 1:
                held = sums[: min(c - 1, tail_from)]
                sent, dkv, held = lax.optimization_barrier((sent, dkv, held))
                sums[: len(held)] = held
                if c - 1 < tail_from:
                    sums[c - 1] = lax.psum_scatter(dkv, "ctx", scatter_dimension=0, tiled=True)
                else:
                    tail = dkv
            received.append(exchange(sent))
        elif 0 <= c - 1 < tail_from:
            sums[c - 1] = lax.psum_scatter(dkv, "ctx", scatter_dimension=0, tiled=True)
        if c < tail_from:
            out, dq, dkv = attend(c, received[c], out, dq, None, sizes[c], 0)
        else:
            done = sum(sizes[tail_from:c])
            out, dq, dkv = attend(c, received[c], out, dq, tail, sum(tail_sizes), done)
            tail = dkv
    sums.append(lax.all_to_all(tail, "ctx", split_axis=0, concat_axis=0, tiled=True))

    dk, dv = pl.pallas_call(
        functools.partial(finish_kernel, sizes[:tail_from] + [sum(tail_sizes)]),
        out_shape=(jax.ShapeDtypeStruct((rows, kv_width), BF16),) * 2,
        compiler_params=params,
        name="finish",
    )(*sums)
    return out, dq, dk, dv


def solution(mesh):
    split = P(("dp", "ctx"), None)
    return jax.shard_map(
        body,
        mesh=mesh,
        in_specs=(
            split,
            split,
            split,
            split,
            P(("dp", "ctx")),
            P("dp", "ctx", None),
            P("dp", "ctx"),
        ),
        out_specs=(split, split, split, split),
        check_vma=False,
    )
```

```python
import functools
import math

import jax
import jax.numpy as jnp
from jax import lax
from jax.experimental import pallas as pl
from jax.experimental.pallas import tpu as pltpu
from jax.sharding import PartitionSpec as P

HD = 128
BLK = 128
F32 = jnp.float32
BF16 = jnp.bfloat16
VMEM_LIMIT = 60 * 1024 * 1024


TAIL = 2


def chunk_sizes(heads):
    if heads < 4:
        return [1] * heads
    half = (heads - TAIL) // 2
    return [half, heads - TAIL - half, 1, 1]


def dot(a, b, ca, cb):
    return lax.dot_general(a, b, (((ca,), (cb,)), ((), ())), preferred_element_type=F32)


def send_order(dest_col, dest_row):
    rows = dest_col.shape[0]
    rank = jnp.sum((dest_col < dest_row).astype(jnp.int32), axis=0, keepdims=True)
    place = lax.broadcasted_iota(jnp.int32, (rows, rows), 0)
    return (place == rank).astype(F32).astype(BF16)


def prep_first_kernel(size, col_ref, row_ref, query_ref, grad_ref, key_ref, value_ref, out_ref):
    rows, width = key_ref.shape
    head_width = query_ref.shape[1] // size
    dest = col_ref[...]
    perm = send_order(dest, row_ref[...])

    def put(at, values):
        out_ref[:, at : at + values.shape[1]] = dot(perm, values, 1, 0).astype(BF16)
        return at + values.shape[1]

    at = 0
    for j in range(size):
        at = put(at, query_ref[:, j * head_width : (j + 1) * head_width])
        at = put(at, grad_ref[:, j * head_width : (j + 1) * head_width])
    at = put(at, key_ref[...])
    at = put(at, value_ref[...])
    slot = jnp.broadcast_to(lax.rem(dest, rows), (rows, HD))
    lane = lax.broadcasted_iota(jnp.int32, (rows, HD), 1)
    put(at, jnp.where(lane == 0, slot & 127, slot >> 7).astype(F32).astype(BF16))


def prep_qg_kernel(col_ref, row_ref, query_ref, grad_ref, out_ref):
    width = query_ref.shape[1]
    perm = send_order(col_ref[...], row_ref[...])
    out_ref[:, 0:width] = dot(perm, query_ref[...], 1, 0).astype(BF16)
    out_ref[:, width:] = dot(perm, grad_ref[...], 1, 0).astype(BF16)


def place_kernel(parts, kv_width, recv_ref, perm_ref, *out_refs):
    rows = perm_ref.shape[0]
    end = recv_ref.shape[1] - HD
    slot = recv_ref[:, end : end + 1].astype(F32) + 128.0 * recv_ref[
        :, end + 1 : end + 2
    ].astype(F32)
    target = lax.broadcasted_iota(jnp.int32, (rows, rows), 1).astype(F32)
    perm = jnp.transpose((target == slot).astype(F32)).astype(BF16)
    perm_ref[...] = perm
    at = end - 2 * kv_width
    for part, out_ref in zip(parts, out_refs):
        width = part * HD
        out_ref[:, 0:width] = dot(perm, recv_ref[:, at : at + width], 1, 0).astype(BF16)
        values = recv_ref[:, at + kv_width : at + kv_width + width]
        out_ref[:, width:] = dot(perm, values, 1, 0).astype(BF16)
        at += width


def finish_kernel(sizes, *refs):
    dk_ref, dv_ref = refs[-2:]
    rows = dk_ref.shape[0]
    head = 0
    for size, ref in zip(sizes, refs):
        total = ref[0:rows, :].astype(F32)
        for part in range(1, ref.shape[0] // rows):
            total = total + ref[part * rows : (part + 1) * rows, :].astype(F32)
        total = total.astype(BF16)
        for j in range(size):
            cols = slice(head * HD, (head + 1) * HD)
            dk_ref[:, cols] = total[:, 2 * j * HD : (2 * j + 1) * HD]
            dv_ref[:, cols] = total[:, (2 * j + 1) * HD : (2 * j + 2) * HD]
            head += 1


def attend_kernel(
    groups, slots, blocks_ref, count_ref, base_ref, perm_ref, qg_ref, key_ref, value_ref, *rest
):
    out_ref, dq_ref, dkv_ref, q_scr, g_scr, dk_scr, dv_scr = rest[-7:]
    rows = perm_ref.shape[0]
    width = groups * HD
    span = slots * BLK
    perm = perm_ref[...]
    q_scr[...] = dot(perm, qg_ref[:, 0:width], 1, 0).astype(BF16)
    g_scr[...] = dot(perm, qg_ref[:, width:], 1, 0).astype(BF16)
    dk_scr[...] = jnp.zeros_like(dk_scr)
    dv_scr[...] = jnp.zeros_like(dv_scr)
    scaling = 1.0 / math.sqrt(HD)
    scale2 = scaling * math.log2(math.e)
    pair = 2
    diff = lax.broadcasted_iota(jnp.int32, (BLK, BLK), 1) - lax.broadcasted_iota(
        jnp.int32, (BLK, BLK), 0
    )
    for b in range(rows // BLK):
        own = base_ref[0] + b
        count = count_ref[b]
        bias, starts = [], []
        for s in range(slots):
            blk = blocks_ref[b * slots + s]
            level = jnp.where(s < count, jnp.where(blk == own, 0, -BLK), BLK)
            bias.append(jnp.where(diff >= level, 0.0, -jnp.inf).astype(F32))
            starts.append(pl.multiple_of(blk * BLK, BLK))
        bias = jnp.concatenate(bias, axis=0)
        bias = jnp.concatenate([bias] * pair, axis=1)
        key_sel = jnp.concatenate([key_ref[pl.ds(at, BLK), :] for at in starts], axis=0)
        value_sel = jnp.concatenate([value_ref[pl.ds(at, BLK), :] for at in starts], axis=0)
        key_t = jnp.transpose(key_sel.astype(F32)).astype(BF16)
        value_t = jnp.transpose(value_sel.astype(F32)).astype(BF16)
        r0 = b * BLK
        dk = jnp.zeros((span, HD), F32)
        dv = jnp.zeros((span, HD), F32)
        for h in range(0, groups, pair):
            cols = [slice((h + i) * HD, (h + i + 1) * HD) for i in range(pair)]
            q2 = jnp.concatenate([q_scr[r0 : r0 + BLK, c] for c in cols], axis=0)
            g2 = jnp.concatenate([g_scr[r0 : r0 + BLK, c] for c in cols], axis=0)
            s_t = dot(key_sel, q2, 1, 1) * scale2 + bias
            dp_t = dot(value_sel, g2, 1, 1)
            e_t = jnp.exp2(s_t - jnp.max(s_t, axis=0, keepdims=True))
            p_t = e_t * (1.0 / jnp.sum(e_t, axis=0, keepdims=True))
            pb_t = p_t.astype(BF16)
            o_t = dot(value_t, pb_t, 1, 0)
            o_low = o_t.astype(BF16).astype(F32)
            delta = jnp.sum(jnp.transpose(g2.astype(F32)) * o_low, axis=0, keepdims=True)
            ds_t = (p_t * (dp_t - delta)).astype(BF16)
            dq_t = dot(key_t, ds_t, 1, 0) * scaling
            o_n = jnp.transpose(o_low).astype(BF16)
            dq_n = jnp.transpose(dq_t).astype(BF16)
            for i, c in enumerate(cols):
                out_ref[r0 : r0 + BLK, c] = o_n[i * BLK : (i + 1) * BLK]
                dq_ref[r0 : r0 + BLK, c] = dq_n[i * BLK : (i + 1) * BLK]
            dk = dk + dot(ds_t, q2, 1, 0)
            dv = dv + dot(pb_t, g2, 1, 0)
        for s, at in enumerate(starts):
            dk_scr[pl.ds(at, BLK), :] += dk[s * BLK : (s + 1) * BLK]
            dv_scr[pl.ds(at, BLK), :] += dv[s * BLK : (s + 1) * BLK]
    dkv_ref[:, 0:HD] = (dk_scr[...] * scaling).astype(BF16)
    dkv_ref[:, HD:] = dv_scr[...].astype(BF16)


def body(query_rows, key_rows, value_rows, grad_out, dest_rows, key_blocks, key_count):
    peers = lax.axis_size("dp") * lax.axis_size("ctx")
    rows, q_width = query_rows.shape
    kv_width = key_rows.shape[1]
    kv_heads = kv_width // HD
    groups = q_width // kv_width
    head_width = groups * HD
    local_blocks, slots = key_blocks.shape[1:]
    seq = rows * lax.axis_size("ctx")
    dest_col = dest_rows.reshape(rows, 1)
    dest_row = dest_rows.reshape(1, rows)
    params = pltpu.CompilerParams(vmem_limit_bytes=VMEM_LIMIT)

    def exchange(x):
        y = lax.all_to_all(
            x.reshape(peers, rows // peers, x.shape[1]),
            ("dp", "ctx"),
            split_axis=0,
            concat_axis=0,
            tiled=True,
        )
        return y.reshape(rows, x.shape[1])

    sizes = chunk_sizes(kv_heads)
    head_cols = sizes[0] * head_width
    sent = pl.pallas_call(
        functools.partial(prep_first_kernel, sizes[0]),
        grid=(1,),
        in_specs=[
            pl.BlockSpec((rows, 1), lambda j: (0, 0)),
            pl.BlockSpec((1, rows), lambda j: (0, 0)),
            pl.BlockSpec((rows, head_cols), lambda j: (0, 0)),
            pl.BlockSpec((rows, head_cols), lambda j: (0, 0)),
            pl.BlockSpec((rows, kv_width), lambda j: (0, 0)),
            pl.BlockSpec((rows, kv_width), lambda j: (0, 0)),
        ],
        out_specs=pl.BlockSpec((rows, 2 * head_cols + 2 * kv_width + HD), lambda j: (0, 0)),
        out_shape=jax.ShapeDtypeStruct((rows, 2 * head_cols + 2 * kv_width + HD), BF16),
        compiler_params=params,
        name="prep_first",
    )(dest_col, dest_row, query_rows, grad_out, key_rows, value_rows)
    received = [exchange(sent)]
    parts = [p for p in (sizes[0], kv_heads - sizes[0]) if p]
    perm, *placed = pl.pallas_call(
        functools.partial(place_kernel, parts, kv_width),
        out_shape=[jax.ShapeDtypeStruct((rows, rows), BF16)]
        + [jax.ShapeDtypeStruct((rows, 2 * part * HD), BF16) for part in parts],
        compiler_params=params,
        name="place_kv",
    )(received[0])
    gathered = [lax.all_gather(x, "ctx", axis=0, tiled=True) for x in placed]

    def send(c):
        first, size = sum(sizes[:c]), sizes[c]
        return pl.pallas_call(
            prep_qg_kernel,
            grid=(size,),
            in_specs=[
                pl.BlockSpec((rows, 1), lambda j: (0, 0)),
                pl.BlockSpec((1, rows), lambda j: (0, 0)),
                pl.BlockSpec((rows, head_width), lambda j: (0, first + j)),
                pl.BlockSpec((rows, head_width), lambda j: (0, first + j)),
            ],
            out_specs=pl.BlockSpec((rows, 2 * head_width), lambda j: (0, j)),
            out_shape=jax.ShapeDtypeStruct((rows, size * 2 * head_width), BF16),
            compiler_params=params,
            cost_estimate=pl.CostEstimate(
                flops=4 * rows * rows * size * head_width,
                bytes_accessed=8 * rows * size * head_width,
                transcendentals=0,
            ),
            name="prep_qg",
        )(dest_col, dest_row, query_rows, grad_out)

    block_list = key_blocks.reshape(local_blocks * slots)
    counts = key_count.reshape(local_blocks)
    base = (lax.axis_index("ctx") * local_blocks).astype(jnp.int32).reshape(1)

    def attend(c, recv, out, dq, dkv, dkv_heads, dkv_first):
        first, size = sum(sizes[:c]), sizes[c]
        which = min(c, 1)
        kv_all = gathered[which]
        head = first - which * sizes[0]
        value_head = parts[which] + head
        operands = [perm, recv, kv_all, kv_all]
        in_specs = [
            pl.BlockSpec((rows, rows), lambda j, *_: (0, 0)),
            pl.BlockSpec((rows, 2 * head_width), lambda j, *_: (0, j)),
            pl.BlockSpec((seq, HD), lambda j, *_: (0, head + j)),
            pl.BlockSpec((seq, HD), lambda j, *_: (0, value_head + j)),
        ]
        aliases = {}
        for place, array in enumerate((out, dq, dkv)):
            if array is not None:
                aliases[3 + len(operands)] = place
                operands.append(array)
                in_specs.append(pl.BlockSpec(memory_space=pl.ANY))
        return pl.pallas_call(
            functools.partial(attend_kernel, groups, slots),
            grid_spec=pltpu.PrefetchScalarGridSpec(
                num_scalar_prefetch=3,
                grid=(size,),
                in_specs=in_specs,
                out_specs=[
                    pl.BlockSpec((rows, head_width), lambda j, *_: (0, first + j)),
                    pl.BlockSpec((rows, head_width), lambda j, *_: (0, first + j)),
                    pl.BlockSpec((seq, 2 * HD), lambda j, *_: (0, dkv_first + j)),
                ],
                scratch_shapes=[
                    pltpu.VMEM((rows, head_width), BF16),
                    pltpu.VMEM((rows, head_width), BF16),
                    pltpu.VMEM((seq, HD), F32),
                    pltpu.VMEM((seq, HD), F32),
                ],
            ),
            out_shape=(
                jax.ShapeDtypeStruct((rows, q_width), BF16),
                jax.ShapeDtypeStruct((rows, q_width), BF16),
                jax.ShapeDtypeStruct((seq, dkv_heads * 2 * HD), BF16),
            ),
            input_output_aliases=aliases,
            compiler_params=params,
            cost_estimate=pl.CostEstimate(
                flops=20 * rows * slots * BLK * size * head_width,
                bytes_accessed=8 * rows * size * head_width + 8 * seq * size * HD,
                transcendentals=rows * slots * BLK * size * groups,
            ),
            name="attend",
        )(block_list, counts, base, *operands)

    chunks = len(sizes)
    tail_from = max(chunks - TAIL, 0)
    tail_sizes = sizes[tail_from:]
    sums = [None] * tail_from
    out = dq = tail = None
    for c in range(chunks):
        if c + 1 < chunks:
            sent = send(c + 1)
            if c >= 1:
                held = sums[: min(c - 1, tail_from)]
                sent, dkv, held, last = lax.optimization_barrier((sent, dkv, held, gathered[-1]))
                gathered[-1] = last
                sums[: len(held)] = held
                if c - 1 < tail_from:
                    sums[c - 1] = lax.psum_scatter(dkv, "ctx", scatter_dimension=0, tiled=True)
                else:
                    tail = dkv
            received.append(exchange(sent))
        elif 0 <= c - 1 < tail_from:
            sums[c - 1] = lax.psum_scatter(dkv, "ctx", scatter_dimension=0, tiled=True)
        if c < tail_from:
            out, dq, dkv = attend(c, received[c], out, dq, None, sizes[c], 0)
        else:
            done = sum(sizes[tail_from:c])
            out, dq, dkv = attend(c, received[c], out, dq, tail, sum(tail_sizes), done)
            tail = dkv
    sums.append(lax.all_to_all(tail, "ctx", split_axis=0, concat_axis=0, tiled=True))

    dk, dv = pl.pallas_call(
        functools.partial(finish_kernel, sizes[:tail_from] + [sum(tail_sizes)]),
        out_shape=(jax.ShapeDtypeStruct((rows, kv_width), BF16),) * 2,
        compiler_params=params,
        name="finish",
    )(*sums)
    return out, dq, dk, dv


def solution(mesh):
    split = P(("dp", "ctx"), None)
    return jax.shard_map(
        body,
        mesh=mesh,
        in_specs=(
            split,
            split,
            split,
            split,
            P(("dp", "ctx")),
            P("dp", "ctx", None),
            P("dp", "ctx"),
        ),
        out_specs=(split, split, split, split),
        check_vma=False,
    )
```
